32 devices in a mesh: rows: 8 (over z, x), batch: 4 (over y, core).
Axes of the slice: x: 2, y: 2, z: 4, core: 2. Of those that a mesh axis runs over, the one named last changes fastest.
Arguments:
- features: bfloat16 [4, 64, 128, 256], P('batch', 'rows'), may hold values from -6 to 6
- kernels: bfloat16 [3, 3, 3, 256, 256], replicated, may hold values from -0.125 to 0.125
- cotangent: bfloat16 [4, 64, 128, 256], P('batch', 'rows'), may hold values from -6 to 6
Outputs:
- result: bfloat16 [4, 64, 128, 256], P('batch', 'rows')
- grad_features: bfloat16 [4, 64, 128, 256], P('batch', 'rows')
- grad_kernels: float32 [3, 3, 3, 256, 256], replicated
The draws below stay inside these ranges and needn't reach their ends.
All inputs are finite; a program needn't handle non-finite values.
Results may differ from the reference program's by a relative error of at most 0.0065.
Values may be sent and summed in bfloat16 or wider, within the bound.
A program may use at most 128 MiB of HBM per device.

```python
import math
import jax
import jax.numpy as jnp
from jax import lax

C = 256
BAND = 8
W = 128
H = 64
B = 4


def level_of(rng, extent, cuts, smallest, top_value):
    level, own = 1.0, jax.random.fold_in(rng, 6)
    for position, parts in cuts:
        heights = jnp.exp(jax.random.uniform(jax.random.fold_in(own, position), (parts,), jnp.float32, smallest / len(cuts), top_value / len(cuts)))
        level = level * jnp.repeat(heights, extent[position] // parts).reshape([-1 if axis == position else 1 for axis in range(len(extent))])
    return level


def gaussian(stream_key, dims, spread, reach, shards=(), held_as=jnp.bfloat16):
    entries = jax.random.normal(stream_key, dims, jnp.float32) * spread
    if len(shards) > 0:
        entries = level_of(stream_key, dims, shards, -0.22, 0.18) * entries
    return jnp.clip(entries, min=-reach, max=reach).astype(held_as)


def setup_inputs(seed: int = 0) -> dict:
    seeds = jax.random.split(jax.random.key(seed), 4)
    features = gaussian(seeds[0], (B, H, W, C), 1.0, 6.0, ((0, 4), (1, 8)))
    kernels = gaussian(seeds[1], (3, 3, 3, C, C), (9 * C) ** -0.5, 0.125)
    cotangent = gaussian(seeds[2], (B, H, W, C), 1.0, 6.0, ((0, 4), (1, 8)))
    return dict(features=features, kernels=kernels, cotangent=cotangent)


def convolve(signal, kernel, dilation):
    return lax.conv_general_dilated(signal, kernel, (1, 1), ((dilation, dilation), (dilation, dilation)), rhs_dilation=(dilation, dilation), dimension_numbers=('NHWC', 'HWIO', 'NHWC'), precision=lax.Precision.HIGHEST)

def activate(values):
    values = values.astype(jnp.float32)
    normed = values * lax.rsqrt(lax.optimization_barrier(jnp.mean(values * values, axis=-1, keepdims=True)) + 1e-05)
    return normed * jax.nn.sigmoid(normed)

def reference(features, kernels, cotangent):
    dilations = [4 * BAND, 8 * BAND, 16 * BAND]
    inputs = []
    current = features
    for layer in range(3):
        inputs.append(current)
        signal = activate(current).astype(jnp.bfloat16)
        conv_out = convolve(signal.astype(jnp.float32), kernels[layer].astype(jnp.float32), dilations[layer])
        current = (current.astype(jnp.float32) + conv_out).astype(jnp.bfloat16)
    result = current
    factor = 1.0 / math.sqrt(features.shape[0] * features.shape[1] * features.shape[2])
    grad_flow = cotangent
    kernel_grads = [None, None, None]
    for layer in [2, 1, 0]:
        signal = lax.optimization_barrier(activate(inputs[layer]).astype(jnp.bfloat16)).astype(jnp.float32)
        dilation = dilations[layer]
        _, pull = jax.vjp(lambda sig, ker: convolve(sig, ker, dilation), signal, kernels[layer].astype(jnp.float32))
        dsignal, dkernel = pull(grad_flow.astype(jnp.float32))
        kernel_grads[layer] = dkernel * factor
        _, back = jax.vjp(activate, inputs[layer].astype(jnp.float32))
        dinput, = back(dsignal)
        grad_flow = (grad_flow.astype(jnp.float32) + dinput).astype(jnp.bfloat16)
    return (result, grad_flow, jnp.stack(kernel_grads))
```

```python
import math

import jax
import jax.numpy as jnp
from jax import lax
from jax.sharding import PartitionSpec as P


def passed_along(value, axis, steps):
    count = lax.axis_size(axis)
    initial, last = (max(0, -steps), min(count, count - steps))
    return lax.ppermute(value, axis, [(source, source + steps) for source in range(initial, last)])


def swapped(value, axis, steps):
    count = lax.axis_size(axis)
    return lax.ppermute(value, axis, [(source, (source + steps) % count) for source in range(count)])


def activate(values):
    values = values.astype(jnp.float32)
    normed = values * lax.rsqrt(jnp.mean(values * values, axis=-1, keepdims=True) + 1e-05)
    return normed * jax.nn.sigmoid(normed)


def shift_columns(array, offset):
    width = array.shape[2]
    reach = abs(offset)
    padded = jnp.pad(array, ((0, 0), (0, 0), (reach, reach), (0, 0)))
    return padded[:, :, reach + offset : reach + offset + width]


def column_taps(width, dilation):
    return [0, 1, 2] if dilation < width else [1]


def tap_forward(source, kernel_row, dilation):
    total = 0.0
    for column in column_taps(source.shape[2], dilation):
        product = jnp.einsum(
            "shwc,cd->shwd", source, kernel_row[column], preferred_element_type=jnp.float32
        )
        total = total + shift_columns(product, (column - 1) * dilation)
    return total


def tap_backward(source, kernel_row, dilation):
    total = 0.0
    for column in column_taps(source.shape[2], dilation):
        product = jnp.einsum(
            "shwd,cd->shwc", source, kernel_row[column], preferred_element_type=jnp.float32
        )
        total = total + shift_columns(product, (1 - column) * dilation)
    return total


def kernel_terms(source, grad_flow, dilation):
    terms = []
    for column in column_taps(source.shape[2], dilation):
        terms.append(
            jnp.einsum(
                "shwc,shwd->cd",
                source,
                shift_columns(grad_flow, (1 - column) * dilation),
                preferred_element_type=jnp.float32,
            )
        )
    return jnp.stack(terms)


def fetch(value, span):
    count = lax.axis_size("rows")
    if span >= count:
        return []
    if 2 * span == count:
        return [(None, swapped(value, "rows", span))]
    return [(0, passed_along(value, "rows", span)), (2, passed_along(value, "rows", -span))]


def local(features, kernels, cotangent):
    band_rows, width = features.shape[1:3]
    count = lax.axis_size("rows")
    spans = [4, 8, 16]
    below = lax.axis_index("rows")
    current = features
    grad_flow = cotangent
    saved = []
    for layer in range(3):
        dilation = spans[layer] * band_rows
        is_lower = below >= spans[layer]
        signal = activate(current).astype(jnp.bfloat16)
        bands = fetch(signal, spans[layer])
        conv_out = tap_forward(signal, kernels[layer, 1], dilation)
        for row, band in bands:
            weights = (
                jnp.where(is_lower, kernels[layer, 0], kernels[layer, 2])
                if row is None
                else kernels[layer, row]
            )
            conv_out = conv_out + tap_forward(band, weights, dilation)
        saved.append((current, signal, bands))
        current = (current.astype(jnp.float32) + conv_out).astype(jnp.bfloat16)
    pixel_count = features.shape[0] * band_rows * width * count * lax.axis_size("batch")
    factor = 1.0 / math.sqrt(pixel_count)
    kernel_grads = [None, None, None]
    for layer in [2, 1, 0]:
        dilation = spans[layer] * band_rows
        is_lower = below >= spans[layer]
        layer_input, signal, bands = saved[layer]
        terms = {1: kernel_terms(signal, grad_flow, dilation)}
        for row, band in bands:
            term = kernel_terms(band, grad_flow, dilation)
            if row is None:
                terms[0] = jnp.where(is_lower, term, 0.0)
                terms[2] = jnp.where(is_lower, 0.0, term)
            else:
                terms[row] = term
        stacked = jnp.stack([terms[row] for row in sorted(terms)]) * factor
        stacked = lax.psum(stacked, ("rows", "batch"))
        wide_r, wide_c = (3 - stacked.shape[0]) // 2, (3 - stacked.shape[1]) // 2
        kernel_grads[layer] = jnp.pad(
            stacked, ((wide_r, wide_r), (wide_c, wide_c), (0, 0), (0, 0))
        )
        dsignal = tap_backward(grad_flow, kernels[layer, 1], dilation)
        for row, band in fetch(grad_flow, spans[layer]):
            weights = (
                jnp.where(is_lower, kernels[layer, 2], kernels[layer, 0])
                if row is None
                else kernels[layer, 2 - row]
            )
            dsignal = dsignal + tap_backward(band, weights, dilation)
        _, back = jax.vjp(activate, layer_input.astype(jnp.float32))
        (dinput,) = back(dsignal)
        grad_flow = (grad_flow.astype(jnp.float32) + dinput).astype(jnp.bfloat16)
    return (current, grad_flow, jnp.stack(kernel_grads))


def solution(mesh):
    placed = (P("batch", "rows", None, None), P(), P("batch", "rows", None, None))
    return jax.shard_map(
        local,
        mesh=mesh,
        in_specs=placed,
        out_specs=(P("batch", "rows", None, None), P("batch", "rows", None, None), P()),
        check_vma=False,
    )
```

```python
import functools
import math

import jax
import jax.numpy as jnp
from jax import lax
from jax.experimental import pallas as pl
from jax.experimental.pallas import tpu as pltpu
from jax.sharding import PartitionSpec as P

SPANS = (4, 8, 16)


def passed_along(value, axis, steps):
    count = lax.axis_size(axis)
    initial, last = (max(0, -steps), min(count, count - steps))
    return lax.ppermute(value, axis, [(source, source + steps) for source in range(initial, last)])


def swapped(value, axis, steps):
    count = lax.axis_size(axis)
    return lax.ppermute(value, axis, [(source, (source + steps) % count) for source in range(count)])


def activate(values):
    values = values.astype(jnp.float32)
    normed = values * lax.rsqrt(jnp.mean(values * values, axis=-1, keepdims=True) + 1e-05)
    return normed * jax.nn.sigmoid(normed)


def shift_columns(array, offset):
    width = array.shape[2]
    reach = abs(offset)
    padded = jnp.pad(array, ((0, 0), (0, 0), (reach, reach), (0, 0)))
    return padded[:, :, reach + offset : reach + offset + width]


def column_taps(width, dilation):
    return [0, 1, 2] if dilation < width else [1]


def tap_forward(source, kernel_row, dilation):
    total = 0.0
    for column in column_taps(source.shape[2], dilation):
        product = jnp.einsum(
            "shwc,cd->shwd", source, kernel_row[column], preferred_element_type=jnp.float32
        )
        total = total + shift_columns(product, (column - 1) * dilation)
    return total


def tap_backward(source, kernel_row, dilation):
    total = 0.0
    for column in column_taps(source.shape[2], dilation):
        product = jnp.einsum(
            "shwd,cd->shwc", source, kernel_row[column], preferred_element_type=jnp.float32
        )
        total = total + shift_columns(product, (1 - column) * dilation)
    return total


def kernel_terms(source, grad_flow, dilation):
    terms = []
    for column in column_taps(source.shape[2], dilation):
        terms.append(
            jnp.einsum(
                "shwc,shwd->cd",
                source,
                shift_columns(grad_flow, (1 - column) * dilation),
                preferred_element_type=jnp.float32,
            )
        )
    return jnp.stack(terms)


def fetch(value, span):
    count = lax.axis_size("rows")
    if span >= count:
        return []
    if 2 * span == count:
        return [(None, swapped(value, "rows", span))]
    return [(0, passed_along(value, "rows", span)), (2, passed_along(value, "rows", -span))]


def local(features, kernels, cotangent):
    band_rows, width = features.shape[1:3]
    count = lax.axis_size("rows")
    spans = SPANS
    below = lax.axis_index("rows")
    current = features
    grad_flow = cotangent
    saved = []
    for layer in range(3):
        dilation = spans[layer] * band_rows
        is_lower = below >= spans[layer]
        signal = activate(current).astype(jnp.bfloat16)
        bands = fetch(signal, spans[layer])
        conv_out = tap_forward(signal, kernels[layer, 1], dilation)
        for row, band in bands:
            weights = (
                jnp.where(is_lower, kernels[layer, 0], kernels[layer, 2])
                if row is None
                else kernels[layer, row]
            )
            conv_out = conv_out + tap_forward(band, weights, dilation)
        saved.append((current, signal, bands))
        current = (current.astype(jnp.float32) + conv_out).astype(jnp.bfloat16)
    pixel_count = features.shape[0] * band_rows * width * count * lax.axis_size("batch")
    factor = 1.0 / math.sqrt(pixel_count)
    kernel_grads = [None, None, None]
    for layer in [2, 1, 0]:
        dilation = spans[layer] * band_rows
        is_lower = below >= spans[layer]
        layer_input, signal, bands = saved[layer]
        terms = {1: kernel_terms(signal, grad_flow, dilation)}
        for row, band in bands:
            term = kernel_terms(band, grad_flow, dilation)
            if row is None:
                terms[0] = jnp.where(is_lower, term, 0.0)
                terms[2] = jnp.where(is_lower, 0.0, term)
            else:
                terms[row] = term
        stacked = jnp.stack([terms[row] for row in sorted(terms)]) * factor
        stacked = lax.psum(stacked, ("rows", "batch"))
        wide_r, wide_c = (3 - stacked.shape[0]) // 2, (3 - stacked.shape[1]) // 2
        kernel_grads[layer] = jnp.pad(
            stacked, ((wide_r, wide_r), (wide_c, wide_c), (0, 0), (0, 0))
        )
        dsignal = tap_backward(grad_flow, kernels[layer, 1], dilation)
        for row, band in fetch(grad_flow, spans[layer]):
            weights = (
                jnp.where(is_lower, kernels[layer, 2], kernels[layer, 0])
                if row is None
                else kernels[layer, 2 - row]
            )
            dsignal = dsignal + tap_backward(band, weights, dilation)
        _, back = jax.vjp(activate, layer_input.astype(jnp.float32))
        (dinput,) = back(dsignal)
        grad_flow = (grad_flow.astype(jnp.float32) + dinput).astype(jnp.bfloat16)
    return (current, grad_flow, jnp.stack(kernel_grads))


MESH = pl.DeviceIdType.MESH
CHUNKS = 4
FLAT = (((1,), (0,)), ((), ()))
TURNED = (((1,), (1,)), ((), ()))
SUMMED = (((0,), (0,)), ((), ()))


def normalise(values):
    scale = lax.rsqrt(jnp.mean(values * values, axis=-1, keepdims=True) + 1e-05)
    normed = values * scale
    gate = 1.0 / (1.0 + jnp.exp(-normed))
    return scale, normed, gate


def activate_back(values, dsignal):
    scale, normed, gate = normalise(values)
    dnormed = dsignal * (gate + normed * gate * (1.0 - gate))
    return scale * (dnormed - normed * jnp.mean(dnormed * normed, axis=-1, keepdims=True))


def moved(array, offset):
    if offset == 0:
        return array
    blank = jnp.zeros((array.shape[0], abs(offset), array.shape[2]), array.dtype)
    if offset > 0:
        return jnp.concatenate([array[:, offset:], blank], axis=1)
    return jnp.concatenate([blank, array[:, :offset]], axis=1)


def flat(array):
    return array.reshape(array.shape[0] * array.shape[1], array.shape[2])


def fused_kernel(
    dilations, features, kernels, cotangent, result, grad_features, gathered,
    weights, signal0, other0, signal1, signal2, flow2, flow1, other1, center, center1,
    parts, from_core, core_sum, from_plane, sum_common, sum_side, from_line, from_side,
    load_sem, swap_send, swap_recv, core_send, core_recv, plane_send, plane_recv,
    line_send, line_recv, side_send, side_recv, gline_send, gline_recv,
    gplane_send, gplane_recv, gcore_send, gcore_recv,
):
    band_rows, width, channels = features.shape
    step = band_rows // CHUNKS
    near, mid = dilations[0], dilations[1]
    row, batch = lax.axis_index("rows"), lax.axis_index("batch")
    line, across = lax.div(row, 2), lax.rem(row, 2)
    plane_y, core = lax.div(batch, 2), lax.rem(batch, 2)
    member = plane_y * 2 + across
    lower = lax.div(line, 2)
    side = lax.rem(line, 2)

    def toggled(value, bits):
        if bits == 1:
            return value + 1 - 2 * lax.rem(value, 2)
        if bits == 2:
            return lax.rem(value + 2, 4)
        return 3 - value

    def on_line(bits):
        return (toggled(line, bits) * 2 + across, batch)

    def on_plane(bits):
        other = toggled(member, bits)
        return (line * 2 + lax.rem(other, 2), lax.div(other, 2) * 2 + core)

    core_mate = (row, plane_y * 2 + 1 - core)
    swap_mate = on_line(2)

    loads = []
    first = 0
    for slot, (tap, taps) in enumerate(((0, 9), (12, 3), (22, 1))):
        copy = pltpu.make_async_copy(
            kernels.at[pl.ds(tap * channels, taps * channels)],
            weights.at[pl.ds(first * channels, taps * channels)],
            load_sem.at[slot],
        )
        copy.start()
        loads.append(copy)
        first += taps

    barrier = pltpu.get_barrier_semaphore()
    mates = [core_mate] + [on_line(k) for k in (1, 2, 3)] + [on_plane(k) for k in (1, 2, 3)]
    for mate in mates:
        pl.semaphore_signal(barrier, inc=1, device_id=mate, device_id_type=MESH)
    pl.semaphore_wait(barrier, len(mates))

    def remote(source, target, send, recv, mate):
        return pltpu.make_async_remote_copy(
            src_ref=source, dst_ref=target, send_sem=send, recv_sem=recv,
            device_id=mate, device_id_type=MESH,
        )

    def swap_signal(k):
        rows = pl.ds(k * step, step)
        return remote(
            signal0.at[rows], other0.at[rows], swap_send.at[k], swap_recv.at[k], swap_mate
        )

    def swap_flow(k):
        rows = pl.ds(k * step, step)
        return remote(
            flow1.at[rows], other1.at[rows],
            swap_send.at[CHUNKS + k], swap_recv.at[CHUNKS + k], swap_mate,
        )

    def dot(left, right, how):
        return lax.dot_general(left, right, how, preferred_element_type=jnp.float32)

    def wide(start):
        if isinstance(start, int):
            return weights[start * channels : (start + 3) * channels]
        return weights[pl.ds(pl.multiple_of(start * channels, channels), 3 * channels)]

    def forward(array, start, dilation):
        return dot(
            jnp.concatenate(
                [flat(moved(array, -dilation)), flat(array), flat(moved(array, dilation))], axis=1
            ),
            wide(start),
            FLAT,
        )

    def backward(array, start, dilation):
        taps = wide(start)
        total = dot(flat(array), taps[channels : 2 * channels], TURNED)
        total = total + dot(flat(moved(array, dilation)), taps[:channels], TURNED)
        return total + dot(flat(moved(array, -dilation)), taps[2 * channels :], TURNED)

    def each_chunk(body):
        def run(k, carry):
            body(k)
            return carry

        lax.fori_loop(0, CHUNKS, run, 0)

    def send_signal(k):
        rows = pl.ds(k * step, step)
        values = flat(features[rows].astype(jnp.float32))
        _, normed, gate = normalise(values)
        signal0[rows] = (normed * gate).astype(jnp.bfloat16).reshape(step, width, channels)
        swap_signal(k).start()

    each_chunk(send_signal)
    loads[0].wait()

    def own_forward(k):
        rows = pl.ds(k * step, step)
        total = forward(signal0[rows], 3, near)
        center[rows] = (flat(features[rows].astype(jnp.float32)) + total).reshape(
            step, width, channels
        )

    each_chunk(own_forward)
    loads[1].wait()
    loads[2].wait()

    def through(k):
        rows = pl.ds(k * step, step)
        shape = (step, width, channels)
        swap_signal(k).wait_recv()
        upper = forward(other0[rows], (1 - lower) * 6, near)
        inner = (flat(center[rows]) + upper).astype(jnp.bfloat16).astype(jnp.float32)
        _, normed, gate = normalise(inner)
        signal = (normed * gate).astype(jnp.bfloat16).reshape(shape)
        signal1[rows] = signal
        deep = (inner + forward(signal, 9, mid)).astype(jnp.bfloat16).astype(jnp.float32)
        _, normed, gate = normalise(deep)
        signal = (normed * gate).astype(jnp.bfloat16)
        signal2[rows] = signal.reshape(shape)
        last = weights[12 * channels : 13 * channels]
        result[rows] = (deep + dot(signal, last, FLAT)).astype(jnp.bfloat16).reshape(shape)
        flow = cotangent[rows]
        dsignal = dot(flat(flow), last, TURNED)
        flow = (flat(flow.astype(jnp.float32)) + activate_back(deep, dsignal)).astype(jnp.bfloat16)
        flow = flow.reshape(shape)
        flow2[rows] = flow
        dsignal = backward(flow, 9, mid)
        flow = flat(flow.astype(jnp.float32)) + activate_back(inner, dsignal)
        flow1[rows] = flow.astype(jnp.bfloat16).reshape(shape)
        swap_flow(k).start()

    each_chunk(through)

    def keep(tap, terms):
        half, quarter = channels // 2, channels // 4
        terms = terms.astype(jnp.bfloat16)
        for h in range(2):
            for q in range(4):
                parts[h, q, tap] = terms[
                    q * quarter : (q + 1) * quarter, h * half : (h + 1) * half
                ]

    def gradient(source, flow, dilation, tap):
        if dilation is None:
            keep(tap, dot(flat(source), flat(flow), SUMMED))
            return
        for c in range(3):
            keep(tap + c, dot(flat(source), flat(moved(flow, (1 - c) * dilation)), SUMMED))

    gradient(signal2[...], cotangent[...], None, 6)
    gradient(signal1[...], flow2[...], mid, 3)
    gradient(signal0[...], flow1[...], near, 0)
    gradient(other0[...], flow1[...], near, 7)

    to_core = remote(parts.at[1 - core], from_core, core_send, core_recv, core_mate)
    to_core.start()

    def own_backward(k):
        rows = pl.ds(k * step, step)
        center1[rows] = backward(flow1[rows], 3, near).reshape(step, width, channels)

    each_chunk(own_backward)

    def finish(k):
        rows = pl.ds(k * step, step)
        swap_flow(k).wait_recv()
        dsignal = flat(center1[rows]) + backward(other1[rows], lower * 6, near)
        flow = flat(flow1[rows].astype(jnp.float32))
        flow = flow + activate_back(flat(features[rows].astype(jnp.float32)), dsignal)
        grad_features[rows] = flow.astype(jnp.bfloat16).reshape(step, width, channels)

    to_core.wait_recv()
    core_sum[...] = (
        parts[core].astype(jnp.float32) + from_core[...].astype(jnp.float32)
    ).astype(jnp.bfloat16)
    to_plane = []
    for k in (1, 2, 3):
        copy = remote(
            core_sum.at[toggled(member, k)], from_plane.at[k - 1],
            plane_send.at[k - 1], plane_recv.at[k - 1], on_plane(k),
        )
        copy.start()
        to_plane.append(copy)

    finish(0)
    for copy in to_plane:
        copy.wait_recv()
    total = core_sum[member].astype(jnp.float32)
    for k in range(3):
        total = total + from_plane[k].astype(jnp.float32)
    total = total.astype(jnp.bfloat16)
    sum_common[...] = total[:7].reshape(sum_common.shape)
    sum_side[...] = total[7:].reshape(sum_side.shape)
    to_line = []
    for k in (1, 2, 3):
        copy = remote(
            sum_common.at[toggled(line, k)], from_line.at[k - 1],
            line_send.at[k - 1], line_recv.at[k - 1], on_line(k),
        )
        copy.start()
        to_line.append(copy)
    to_side = remote(sum_side.at[1 - side], from_side, side_send, side_recv, on_line(1))
    to_side.start()

    finish(1)
    for copy in to_line:
        copy.wait_recv()
    to_side.wait_recv()
    common = sum_common.shape[1]
    total = sum_common[line].astype(jnp.float32)
    for k in range(3):
        total = total + from_line[k].astype(jnp.float32)
    mine = gathered.at[core, member, line]
    mine[:common] = total.astype(jnp.bfloat16)
    total = sum_side[side].astype(jnp.float32) + from_side[...].astype(jnp.float32)
    mine[common:] = total.astype(jnp.bfloat16)

    along_line = []
    for k in (1, 2, 3):
        copy = remote(mine, mine, gline_send.at[k - 1], gline_recv.at[k - 1], on_line(k))
        copy.start()
        along_line.append(copy)
    finish(2)
    for copy in along_line:
        copy.wait_recv()
    quarter = gathered.at[core, member]
    across_core = []
    across_plane = []
    for k in (1, 2, 3):
        copy = remote(quarter, quarter, gplane_send.at[k - 1], gplane_recv.at[k - 1], on_plane(k))
        copy.start()
        across_plane.append(copy)
    copy = remote(quarter, quarter, gcore_send.at[0], gcore_recv.at[0], core_mate)
    copy.start()
    across_core.append(copy)
    finish(3)
    for k in (1, 2, 3):
        across_plane[k - 1].wait_recv()
        piece = gathered.at[core, toggled(member, k)]
        copy = remote(piece, piece, gcore_send.at[k], gcore_recv.at[k], core_mate)
        copy.start()
        across_core.append(copy)
    for copy in across_core:
        copy.wait_recv()
    for copy in [to_core, to_side] + to_plane + to_line + along_line + across_plane + across_core:
        copy.wait_send()

    def sent(k):
        swap_signal(k).wait_send()
        swap_flow(k).wait_send()

    each_chunk(sent)


def fused(features, kernels, cotangent):
    samples, band_rows, width, channels = features.shape
    dilations = [span * band_rows for span in SPANS]
    band = (band_rows, width, channels)
    low, full = jnp.bfloat16, jnp.float32
    half, quarter = channels // 2, channels // 4
    common, sides = 7 * quarter // 4, 3 * quarter // 2
    dma = pltpu.SemaphoreType.DMA
    vmem = pltpu.VMEM
    whole = pl.BlockSpec(memory_space=pltpu.VMEM)
    result, grad_features, gathered = pl.pallas_call(
        functools.partial(fused_kernel, dilations),
        out_shape=(
            jax.ShapeDtypeStruct(band, low),
            jax.ShapeDtypeStruct(band, low),
            jax.ShapeDtypeStruct((2, 4, 4, common + sides, half), low),
        ),
        in_specs=[whole, pl.BlockSpec(memory_space=pl.ANY), whole],
        out_specs=(whole, whole, whole),
        scratch_shapes=[
            vmem((13 * channels, channels), low),
            *[vmem(band, low) for _ in range(7)],
            vmem(band, full),
            vmem(band, full),
            vmem((2, 4, 10, quarter, half), low),
            vmem((4, 10, quarter, half), low),
            vmem((4, 10, quarter, half), low),
            vmem((3, 10, quarter, half), low),
            vmem((4, common, half), low),
            vmem((2, sides, half), low),
            vmem((3, common, half), low),
            vmem((sides, half), low),
            dma((3,)),
            dma((2 * CHUNKS,)),
            dma((2 * CHUNKS,)),
            dma, dma,
            dma((3,)), dma((3,)),
            dma((3,)), dma((3,)),
            dma, dma,
            dma((3,)), dma((3,)),
            dma((3,)), dma((3,)),
            dma((4,)), dma((4,)),
        ],
        compiler_params=pltpu.CompilerParams(
            collective_id=0, has_side_effects=True, vmem_limit_bytes=48 * 2**20
        ),
        cost_estimate=pl.CostEstimate(
            flops=48 * band_rows * width * channels * channels,
            bytes_accessed=10 * band_rows * width * channels,
            transcendentals=8 * band_rows * width * channels,
        ),
    )(
        features.reshape(band),
        kernels.reshape(27 * channels, channels),
        cotangent.reshape(band),
    )
    cells = samples * band_rows * width * lax.axis_size("rows") * lax.axis_size("batch")
    factor = 1.0 / math.sqrt(cells)
    terms = gathered.astype(full) * factor
    inner = terms[:, :, :, :common].reshape(2, 4, 7, quarter, half)
    inner = jnp.transpose(inner, (2, 1, 3, 0, 4)).reshape(7, channels, channels)
    outer = terms[:, :, :, common:].reshape(2, 4, 2, 3, quarter, half)
    outer = jnp.transpose(outer, (2, 3, 1, 4, 0, 5)).reshape(2, 3, channels, channels)
    first = jnp.stack([outer[1], inner[0:3], outer[0]])
    second = jnp.pad(inner[3:6][None], ((1, 1), (0, 0), (0, 0), (0, 0)))
    third = jnp.pad(inner[6:7][None], ((1, 1), (1, 1), (0, 0), (0, 0)))
    return (
        result.reshape(features.shape),
        grad_features.reshape(features.shape),
        jnp.stack([first, second, third]),
    )


def one_swap(features):
    band_rows, width, channels = features.shape[1:]
    dilations = [span * band_rows for span in SPANS]
    return (
        features.shape[0] == 1
        and lax.axis_size("rows") == 2 * SPANS[0]
        and lax.axis_size("batch") == 4
        and SPANS[1] >= 2 * SPANS[0]
        and dilations[1] < width <= dilations[2]
        and band_rows % CHUNKS == 0
        and channels == 256
    )


def device_part(features, kernels, cotangent):
    if one_swap(features):
        return fused(features, kernels, cotangent)
    return local(features, kernels, cotangent)


def solution(mesh):
    placed = (P("batch", "rows", None, None), P(), P("batch", "rows", None, None))
    return jax.shard_map(
        device_part,
        mesh=mesh,
        in_specs=placed,
        out_specs=(P("batch", "rows", None, None), P("batch", "rows", None, None), P()),
        check_vma=False,
    )
```

```python
import functools
import math

import jax
import jax.numpy as jnp
from jax import lax
from jax.experimental import pallas as pl
from jax.experimental.pallas import tpu as pltpu
from jax.sharding import PartitionSpec as P

SPANS = (4, 8, 16)


def passed_along(value, axis, steps):
    count = lax.axis_size(axis)
    initial, last = (max(0, -steps), min(count, count - steps))
    return lax.ppermute(value, axis, [(source, source + steps) for source in range(initial, last)])


def swapped(value, axis, steps):
    count = lax.axis_size(axis)
    return lax.ppermute(value, axis, [(source, (source + steps) % count) for source in range(count)])


def activate(values):
    values = values.astype(jnp.float32)
    normed = values * lax.rsqrt(jnp.mean(values * values, axis=-1, keepdims=True) + 1e-05)
    return normed * jax.nn.sigmoid(normed)


def shift_columns(array, offset):
    width = array.shape[2]
    reach = abs(offset)
    padded = jnp.pad(array, ((0, 0), (0, 0), (reach, reach), (0, 0)))
    return padded[:, :, reach + offset : reach + offset + width]


def column_taps(width, dilation):
    return [0, 1, 2] if dilation < width else [1]


def tap_forward(source, kernel_row, dilation):
    total = 0.0
    for column in column_taps(source.shape[2], dilation):
        product = jnp.einsum(
            "shwc,cd->shwd", source, kernel_row[column], preferred_element_type=jnp.float32
        )
        total = total + shift_columns(product, (column - 1) * dilation)
    return total


def tap_backward(source, kernel_row, dilation):
    total = 0.0
    for column in column_taps(source.shape[2], dilation):
        product = jnp.einsum(
            "shwd,cd->shwc", source, kernel_row[column], preferred_element_type=jnp.float32
        )
        total = total + shift_columns(product, (1 - column) * dilation)
    return total


def kernel_terms(source, grad_flow, dilation):
    terms = []
    for column in column_taps(source.shape[2], dilation):
        terms.append(
            jnp.einsum(
                "shwc,shwd->cd",
                source,
                shift_columns(grad_flow, (1 - column) * dilation),
                preferred_element_type=jnp.float32,
            )
        )
    return jnp.stack(terms)


def fetch(value, span):
    count = lax.axis_size("rows")
    if span >= count:
        return []
    if 2 * span == count:
        return [(None, swapped(value, "rows", span))]
    return [(0, passed_along(value, "rows", span)), (2, passed_along(value, "rows", -span))]


def local(features, kernels, cotangent):
    band_rows, width = features.shape[1:3]
    count = lax.axis_size("rows")
    spans = SPANS
    below = lax.axis_index("rows")
    current = features
    grad_flow = cotangent
    saved = []
    for layer in range(3):
        dilation = spans[layer] * band_rows
        is_lower = below >= spans[layer]
        signal = activate(current).astype(jnp.bfloat16)
        bands = fetch(signal, spans[layer])
        conv_out = tap_forward(signal, kernels[layer, 1], dilation)
        for row, band in bands:
            weights = (
                jnp.where(is_lower, kernels[layer, 0], kernels[layer, 2])
                if row is None
                else kernels[layer, row]
            )
            conv_out = conv_out + tap_forward(band, weights, dilation)
        saved.append((current, signal, bands))
        current = (current.astype(jnp.float32) + conv_out).astype(jnp.bfloat16)
    pixel_count = features.shape[0] * band_rows * width * count * lax.axis_size("batch")
    factor = 1.0 / math.sqrt(pixel_count)
    kernel_grads = [None, None, None]
    for layer in [2, 1, 0]:
        dilation = spans[layer] * band_rows
        is_lower = below >= spans[layer]
        layer_input, signal, bands = saved[layer]
        terms = {1: kernel_terms(signal, grad_flow, dilation)}
        for row, band in bands:
            term = kernel_terms(band, grad_flow, dilation)
            if row is None:
                terms[0] = jnp.where(is_lower, term, 0.0)
                terms[2] = jnp.where(is_lower, 0.0, term)
            else:
                terms[row] = term
        stacked = jnp.stack([terms[row] for row in sorted(terms)]) * factor
        stacked = lax.psum(stacked, ("rows", "batch"))
        wide_r, wide_c = (3 - stacked.shape[0]) // 2, (3 - stacked.shape[1]) // 2
        kernel_grads[layer] = jnp.pad(
            stacked, ((wide_r, wide_r), (wide_c, wide_c), (0, 0), (0, 0))
        )
        dsignal = tap_backward(grad_flow, kernels[layer, 1], dilation)
        for row, band in fetch(grad_flow, spans[layer]):
            weights = (
                jnp.where(is_lower, kernels[layer, 2], kernels[layer, 0])
                if row is None
                else kernels[layer, 2 - row]
            )
            dsignal = dsignal + tap_backward(band, weights, dilation)
        _, back = jax.vjp(activate, layer_input.astype(jnp.float32))
        (dinput,) = back(dsignal)
        grad_flow = (grad_flow.astype(jnp.float32) + dinput).astype(jnp.bfloat16)
    return (current, grad_flow, jnp.stack(kernel_grads))


MESH = pl.DeviceIdType.MESH
CHUNKS = 4
FLAT = (((1,), (0,)), ((), ()))
TURNED = (((1,), (1,)), ((), ()))
SUMMED = (((0,), (0,)), ((), ()))


def normalise(values):
    scale = lax.rsqrt(jnp.mean(values * values, axis=-1, keepdims=True) + 1e-05)
    normed = values * scale
    gate = 1.0 / (1.0 + jnp.exp(-normed))
    return scale, normed, gate


def activate_back(values, dsignal):
    scale, normed, gate = normalise(values)
    dnormed = dsignal * (gate + normed * gate * (1.0 - gate))
    return scale * (dnormed - normed * jnp.mean(dnormed * normed, axis=-1, keepdims=True))


def moved(array, offset):
    if offset == 0:
        return array
    blank = jnp.zeros((array.shape[0], abs(offset), array.shape[2]), array.dtype)
    if offset > 0:
        return jnp.concatenate([array[:, offset:], blank], axis=1)
    return jnp.concatenate([blank, array[:, :offset]], axis=1)


def flat(array):
    return array.reshape(array.shape[0] * array.shape[1], array.shape[2])


def fused_kernel(
    dilations, features, kernels, cotangent, result, grad_features, gathered,
    weights, signal0, other0, signal1, signal2, flow2, flow1, other1, center, center1,
    parts, from_core, core_sum, from_plane, sum_common, sum_side, from_line, from_side,
    load_sem, swap_send, swap_recv, core_send, core_recv, plane_send, plane_recv,
    line_send, line_recv, side_send, side_recv, gline_send, gline_recv,
    gplane_send, gplane_recv, gcore_send, gcore_recv,
):
    band_rows, width, channels = features.shape
    step = band_rows // CHUNKS
    near, mid = dilations[0], dilations[1]
    row, batch = lax.axis_index("rows"), lax.axis_index("batch")
    line, across = lax.div(row, 2), lax.rem(row, 2)
    plane_y, core = lax.div(batch, 2), lax.rem(batch, 2)
    member = plane_y * 2 + across
    lower = lax.div(line, 2)
    side = lax.rem(line, 2)

    def toggled(value, bits):
        if bits == 1:
            return value + 1 - 2 * lax.rem(value, 2)
        if bits == 2:
            return lax.rem(value + 2, 4)
        return 3 - value

    def on_line(bits):
        return (toggled(line, bits) * 2 + across, batch)

    def on_plane(bits):
        other = toggled(member, bits)
        return (line * 2 + lax.rem(other, 2), lax.div(other, 2) * 2 + core)

    core_mate = (row, plane_y * 2 + 1 - core)
    swap_mate = on_line(2)

    loads = []
    first = 0
    for slot, (tap, taps) in enumerate(((0, 9), (12, 3), (22, 1))):
        copy = pltpu.make_async_copy(
            kernels.at[pl.ds(tap * channels, taps * channels)],
            weights.at[pl.ds(first * channels, taps * channels)],
            load_sem.at[slot],
        )
        copy.start()
        loads.append(copy)
        first += taps

    barrier = pltpu.get_barrier_semaphore()
    mates = [core_mate] + [on_line(k) for k in (1, 2, 3)] + [on_plane(k) for k in (1, 2, 3)]
    for mate in mates:
        pl.semaphore_signal(barrier, inc=1, device_id=mate, device_id_type=MESH)
    pl.semaphore_wait(barrier, len(mates))

    def remote(source, target, send, recv, mate):
        return pltpu.make_async_remote_copy(
            src_ref=source, dst_ref=target, send_sem=send, recv_sem=recv,
            device_id=mate, device_id_type=MESH,
        )

    def swap_signal(k):
        rows = pl.ds(k * step, step)
        return remote(
            signal0.at[rows], other0.at[rows], swap_send.at[k], swap_recv.at[k], swap_mate
        )

    def swap_flow(k):
        rows = pl.ds(k * step, step)
        return remote(
            flow1.at[rows], other1.at[rows],
            swap_send.at[CHUNKS + k], swap_recv.at[CHUNKS + k], swap_mate,
        )

    def dot(left, right, how):
        return lax.dot_general(left, right, how, preferred_element_type=jnp.float32)

    def wide(start):
        if isinstance(start, int):
            return weights[start * channels : (start + 3) * channels]
        return weights[pl.ds(pl.multiple_of(start * channels, channels), 3 * channels)]

    def forward(array, start, dilation):
        return dot(
            jnp.concatenate(
                [flat(moved(array, -dilation)), flat(array), flat(moved(array, dilation))], axis=1
            ),
            wide(start),
            FLAT,
        )

    def backward(array, start, dilation):
        taps = wide(start)
        total = dot(flat(array), taps[channels : 2 * channels], TURNED)
        total = total + dot(flat(moved(array, dilation)), taps[:channels], TURNED)
        return total + dot(flat(moved(array, -dilation)), taps[2 * channels :], TURNED)

    def each_chunk(body):
        def run(k, carry):
            body(k)
            return carry

        lax.fori_loop(0, CHUNKS, run, 0)

    def send_signal(k):
        rows = pl.ds(k * step, step)
        values = flat(features[rows].astype(jnp.float32))
        _, normed, gate = normalise(values)
        signal0[rows] = (normed * gate).astype(jnp.bfloat16).reshape(step, width, channels)
        swap_signal(k).start()

    each_chunk(send_signal)
    loads[0].wait()

    def own_forward(k):
        rows = pl.ds(k * step, step)
        total = forward(signal0[rows], 3, near)
        center[rows] = (flat(features[rows].astype(jnp.float32)) + total).reshape(
            step, width, channels
        )

    each_chunk(own_forward)
    loads[1].wait()
    loads[2].wait()

    def through(k):
        rows = pl.ds(k * step, step)
        shape = (step, width, channels)
        swap_signal(k).wait_recv()
        upper = forward(other0[rows], (1 - lower) * 6, near)
        inner = (flat(center[rows]) + upper).astype(jnp.bfloat16).astype(jnp.float32)
        _, normed, gate = normalise(inner)
        signal = (normed * gate).astype(jnp.bfloat16).reshape(shape)
        signal1[rows] = signal
        deep = (inner + forward(signal, 9, mid)).astype(jnp.bfloat16).astype(jnp.float32)
        _, normed, gate = normalise(deep)
        signal = (normed * gate).astype(jnp.bfloat16)
        signal2[rows] = signal.reshape(shape)
        last = weights[12 * channels : 13 * channels]
        result[rows] = (deep + dot(signal, last, FLAT)).astype(jnp.bfloat16).reshape(shape)
        flow = cotangent[rows]
        dsignal = dot(flat(flow), last, TURNED)
        flow = (flat(flow.astype(jnp.float32)) + activate_back(deep, dsignal)).astype(jnp.bfloat16)
        flow = flow.reshape(shape)
        flow2[rows] = flow
        dsignal = backward(flow, 9, mid)
        flow = flat(flow.astype(jnp.float32)) + activate_back(inner, dsignal)
        flow1[rows] = flow.astype(jnp.bfloat16).reshape(shape)
        swap_flow(k).start()

    each_chunk(through)

    def keep(tap, terms):
        half, quarter = channels // 2, channels // 4
        terms = terms.astype(jnp.bfloat16)
        for h in range(2):
            for q in range(4):
                parts[h, q, tap] = terms[
                    q * quarter : (q + 1) * quarter, h * half : (h + 1) * half
                ]

    def gradient(source, flow, dilation, tap):
        if dilation is None:
            keep(tap, dot(flat(source), flat(flow), SUMMED))
            return
        for c in range(3):
            keep(tap + c, dot(flat(source), flat(moved(flow, (1 - c) * dilation)), SUMMED))

    gradient(signal2[...], cotangent[...], None, 6)
    gradient(signal1[...], flow2[...], mid, 3)
    gradient(signal0[...], flow1[...], near, 0)
    gradient(other0[...], flow1[...], near, 7)

    to_core = remote(parts.at[1 - core], from_core, core_send, core_recv, core_mate)
    to_core.start()

    def own_backward(k):
        rows = pl.ds(k * step, step)
        center1[rows] = backward(flow1[rows], 3, near).reshape(step, width, channels)

    each_chunk(own_backward)

    def finish(k):
        rows = pl.ds(k * step, step)
        swap_flow(k).wait_recv()
        dsignal = flat(center1[rows]) + backward(other1[rows], lower * 6, near)
        flow = flat(flow1[rows].astype(jnp.float32))
        flow = flow + activate_back(flat(features[rows].astype(jnp.float32)), dsignal)
        grad_features[rows] = flow.astype(jnp.bfloat16).reshape(step, width, channels)

    to_core.wait_recv()
    core_sum[...] = (
        parts[core].astype(jnp.float32) + from_core[...].astype(jnp.float32)
    ).astype(jnp.bfloat16)
    to_plane = []
    for k in (1, 2, 3):
        copy = remote(
            core_sum.at[toggled(member, k)], from_plane.at[k - 1],
            plane_send.at[k - 1], plane_recv.at[k - 1], on_plane(k),
        )
        copy.start()
        to_plane.append(copy)

    finish(0)
    for copy in to_plane:
        copy.wait_recv()
    total = core_sum[member].astype(jnp.float32)
    for k in range(3):
        total = total + from_plane[k].astype(jnp.float32)
    total = total.astype(jnp.bfloat16)
    sum_common[...] = total[:7].reshape(sum_common.shape)
    sum_side[...] = total[7:].reshape(sum_side.shape)
    to_line = []
    for k in (1, 2, 3):
        copy = remote(
            sum_common.at[toggled(line, k)], from_line.at[k - 1],
            line_send.at[k - 1], line_recv.at[k - 1], on_line(k),
        )
        copy.start()
        to_line.append(copy)
    to_side = remote(sum_side.at[1 - side], from_side, side_send, side_recv, on_line(1))
    to_side.start()

    finish(1)
    for copy in to_line:
        copy.wait_recv()
    to_side.wait_recv()
    common = sum_common.shape[1]
    total = sum_common[line].astype(jnp.float32)
    for k in range(3):
        total = total + from_line[k].astype(jnp.float32)
    mine = gathered.at[core, member, line]
    mine[:common] = total.astype(jnp.bfloat16)
    total = sum_side[side].astype(jnp.float32) + from_side[...].astype(jnp.float32)
    mine[common:] = total.astype(jnp.bfloat16)

    along_line = []
    for k in (1, 2, 3):
        copy = remote(mine, mine, gline_send.at[k - 1], gline_recv.at[k - 1], on_line(k))
        copy.start()
        along_line.append(copy)
    finish(2)
    for copy in along_line:
        copy.wait_recv()
    quarter = gathered.at[core, member]
    across_core = []
    across_plane = []
    for k in (1, 2, 3):
        copy = remote(quarter, quarter, gplane_send.at[k - 1], gplane_recv.at[k - 1], on_plane(k))
        copy.start()
        across_plane.append(copy)
    copy = remote(quarter, quarter, gcore_send.at[0], gcore_recv.at[0], core_mate)
    copy.start()
    across_core.append(copy)
    finish(3)
    for k in (1, 2, 3):
        across_plane[k - 1].wait_recv()
        piece = gathered.at[core, toggled(member, k)]
        copy = remote(piece, piece, gcore_send.at[k], gcore_recv.at[k], core_mate)
        copy.start()
        across_core.append(copy)
    for copy in across_core:
        copy.wait_recv()
    for copy in [to_core, to_side] + to_plane + to_line + along_line + across_plane + across_core:
        copy.wait_send()

    def sent(k):
        swap_signal(k).wait_send()
        swap_flow(k).wait_send()

    each_chunk(sent)


def spread_kernel(
    factor, gathered, result, grad_features, out_result, out_features, out_kernels,
    pieces, sems,
):
    copies = [
        pltpu.make_async_copy(result, out_result, sems.at[0]),
        pltpu.make_async_copy(grad_features, out_features, sems.at[1]),
    ]
    for copy in copies:
        copy.start()
    quarter, half = gathered.shape[3] * 4 // 13, gathered.shape[4]
    common = 7 * quarter // 4
    sides = 3 * quarter // 2
    places = [None] * 13
    for tap in range(3):
        places[tap] = 3 + tap
        places[3 + tap] = 12 + tap
        places[7 + tap] = 6 + tap
        places[10 + tap] = tap
    places[6] = 22
    blank = pieces.at[13:16]
    blank[...] = jnp.zeros(blank.shape, jnp.float32)
    zeros = [(9, 3), (15, 3), (18, 3), (21, 1), (23, 1), (24, 3)]
    for slot, (tap, taps) in enumerate(zeros):
        copies.append(
            pltpu.make_async_copy(
                blank.at[:taps], out_kernels.at[pl.ds(tap, taps)], sems.at[2 + slot]
            )
        )
        copies[-1].start()
    for tap in range(13):
        for q in range(4):
            done = 0
            while done < quarter:
                if tap < 7:
                    spot, size = tap * quarter + done, common
                    line, start = spot // size, spot % size
                    offset = 0
                else:
                    upper, inner = (tap - 7) // 3, (tap - 7) % 3
                    spot, size = inner * quarter + done, sides
                    line, start = 2 * upper + spot // size, spot % size
                    offset = common
                rows = min(quarter - done, size - start)
                for h in range(2):
                    block = gathered[h, q, line, offset + start : offset + start + rows]
                    pieces[
                        tap,
                        q * quarter + done : q * quarter + done + rows,
                        h * half : (h + 1) * half,
                    ] = block.astype(jnp.float32) * factor
                done += rows
        copies.append(
            pltpu.make_async_copy(pieces.at[tap], out_kernels.at[places[tap]], sems.at[8 + tap])
        )
        copies[-1].start()
    for copy in copies:
        copy.wait()


def fused(features, kernels, cotangent):
    samples, band_rows, width, channels = features.shape
    dilations = [span * band_rows for span in SPANS]
    band = (band_rows, width, channels)
    low, full = jnp.bfloat16, jnp.float32
    half, quarter = channels // 2, channels // 4
    common, sides = 7 * quarter // 4, 3 * quarter // 2
    dma = pltpu.SemaphoreType.DMA
    vmem = pltpu.VMEM
    whole = pl.BlockSpec(memory_space=pltpu.VMEM)
    result, grad_features, gathered = pl.pallas_call(
        functools.partial(fused_kernel, dilations),
        out_shape=(
            jax.ShapeDtypeStruct(band, low),
            jax.ShapeDtypeStruct(band, low),
            jax.ShapeDtypeStruct((2, 4, 4, common + sides, half), low),
        ),
        in_specs=[whole, pl.BlockSpec(memory_space=pl.ANY), whole],
        out_specs=(whole, whole, whole),
        scratch_shapes=[
            vmem((13 * channels, channels), low),
            *[vmem(band, low) for _ in range(7)],
            vmem(band, full),
            vmem(band, full),
            vmem((2, 4, 10, quarter, half), low),
            vmem((4, 10, quarter, half), low),
            vmem((4, 10, quarter, half), low),
            vmem((3, 10, quarter, half), low),
            vmem((4, common, half), low),
            vmem((2, sides, half), low),
            vmem((3, common, half), low),
            vmem((sides, half), low),
            dma((3,)),
            dma((2 * CHUNKS,)),
            dma((2 * CHUNKS,)),
            dma, dma,
            dma((3,)), dma((3,)),
            dma((3,)), dma((3,)),
            dma, dma,
            dma((3,)), dma((3,)),
            dma((3,)), dma((3,)),
            dma((4,)), dma((4,)),
        ],
        compiler_params=pltpu.CompilerParams(
            collective_id=0, has_side_effects=True, vmem_limit_bytes=48 * 2**20
        ),
        cost_estimate=pl.CostEstimate(
            flops=48 * band_rows * width * channels * channels,
            bytes_accessed=10 * band_rows * width * channels,
            transcendentals=8 * band_rows * width * channels,
        ),
    )(
        features.reshape(band),
        kernels.reshape(27 * channels, channels),
        cotangent.reshape(band),
    )
    cells = samples * band_rows * width * lax.axis_size("rows") * lax.axis_size("batch")
    factor = 1.0 / math.sqrt(cells)
    anywhere = pl.BlockSpec(memory_space=pl.ANY)
    result, grad_features, terms = pl.pallas_call(
        functools.partial(spread_kernel, factor),
        out_shape=(
            jax.ShapeDtypeStruct(band, low),
            jax.ShapeDtypeStruct(band, low),
            jax.ShapeDtypeStruct((27, channels, channels), full),
        ),
        in_specs=[whole, anywhere, anywhere],
        out_specs=(anywhere, anywhere, anywhere),
        scratch_shapes=[vmem((16, channels, channels), full), dma((21,))],
        compiler_params=pltpu.CompilerParams(vmem_limit_bytes=16 * 2**20),
    )(gathered, result, grad_features)
    return (
        result.reshape(features.shape),
        grad_features.reshape(features.shape),
        terms.reshape(3, 3, 3, channels, channels),
    )


def one_swap(features):
    band_rows, width, channels = features.shape[1:]
    dilations = [span * band_rows for span in SPANS]
    return (
        features.shape[0] == 1
        and lax.axis_size("rows") == 2 * SPANS[0]
        and lax.axis_size("batch") == 4
        and SPANS[1] >= 2 * SPANS[0]
        and dilations[1] < width <= dilations[2]
        and band_rows % CHUNKS == 0
        and channels == 256
    )


def device_part(features, kernels, cotangent):
    if one_swap(features):
        return fused(features, kernels, cotangent)
    return local(features, kernels, cotangent)


def solution(mesh):
    placed = (P("batch", "rows", None, None), P(), P("batch", "rows", None, None))
    return jax.shard_map(
        device_part,
        mesh=mesh,
        in_specs=placed,
        out_specs=(P("batch", "rows", None, None), P("batch", "rows", None, None), P()),
        check_vma=False,
    )
```

```python
import functools
import math

import jax
import jax.numpy as jnp
from jax import lax
from jax.experimental import pallas as pl
from jax.experimental.pallas import tpu as pltpu
from jax.sharding import PartitionSpec as P

SPANS = (4, 8, 16)


def passed_along(value, axis, steps):
    count = lax.axis_size(axis)
    initial, last = (max(0, -steps), min(count, count - steps))
    return lax.ppermute(value, axis, [(source, source + steps) for source in range(initial, last)])


def swapped(value, axis, steps):
    count = lax.axis_size(axis)
    return lax.ppermute(value, axis, [(source, (source + steps) % count) for source in range(count)])


def activate(values):
    values = values.astype(jnp.float32)
    normed = values * lax.rsqrt(jnp.mean(values * values, axis=-1, keepdims=True) + 1e-05)
    return normed * jax.nn.sigmoid(normed)


def shift_columns(array, offset):
    width = array.shape[2]
    reach = abs(offset)
    padded = jnp.pad(array, ((0, 0), (0, 0), (reach, reach), (0, 0)))
    return padded[:, :, reach + offset : reach + offset + width]


def column_taps(width, dilation):
    return [0, 1, 2] if dilation < width else [1]


def tap_forward(source, kernel_row, dilation):
    total = 0.0
    for column in column_taps(source.shape[2], dilation):
        product = jnp.einsum(
            "shwc,cd->shwd", source, kernel_row[column], preferred_element_type=jnp.float32
        )
        total = total + shift_columns(product, (column - 1) * dilation)
    return total


def tap_backward(source, kernel_row, dilation):
    total = 0.0
    for column in column_taps(source.shape[2], dilation):
        product = jnp.einsum(
            "shwd,cd->shwc", source, kernel_row[column], preferred_element_type=jnp.float32
        )
        total = total + shift_columns(product, (1 - column) * dilation)
    return total


def kernel_terms(source, grad_flow, dilation):
    terms = []
    for column in column_taps(source.shape[2], dilation):
        terms.append(
            jnp.einsum(
                "shwc,shwd->cd",
                source,
                shift_columns(grad_flow, (1 - column) * dilation),
                preferred_element_type=jnp.float32,
            )
        )
    return jnp.stack(terms)


def fetch(value, span):
    count = lax.axis_size("rows")
    if span >= count:
        return []
    if 2 * span == count:
        return [(None, swapped(value, "rows", span))]
    return [(0, passed_along(value, "rows", span)), (2, passed_along(value, "rows", -span))]


def local(features, kernels, cotangent):
    band_rows, width = features.shape[1:3]
    count = lax.axis_size("rows")
    spans = SPANS
    below = lax.axis_index("rows")
    current = features
    grad_flow = cotangent
    saved = []
    for layer in range(3):
        dilation = spans[layer] * band_rows
        is_lower = below >= spans[layer]
        signal = activate(current).astype(jnp.bfloat16)
        bands = fetch(signal, spans[layer])
        conv_out = tap_forward(signal, kernels[layer, 1], dilation)
        for row, band in bands:
            weights = (
                jnp.where(is_lower, kernels[layer, 0], kernels[layer, 2])
                if row is None
                else kernels[layer, row]
            )
            conv_out = conv_out + tap_forward(band, weights, dilation)
        saved.append((current, signal, bands))
        current = (current.astype(jnp.float32) + conv_out).astype(jnp.bfloat16)
    pixel_count = features.shape[0] * band_rows * width * count * lax.axis_size("batch")
    factor = 1.0 / math.sqrt(pixel_count)
    kernel_grads = [None, None, None]
    for layer in [2, 1, 0]:
        dilation = spans[layer] * band_rows
        is_lower = below >= spans[layer]
        layer_input, signal, bands = saved[layer]
        terms = {1: kernel_terms(signal, grad_flow, dilation)}
        for row, band in bands:
            term = kernel_terms(band, grad_flow, dilation)
            if row is None:
                terms[0] = jnp.where(is_lower, term, 0.0)
                terms[2] = jnp.where(is_lower, 0.0, term)
            else:
                terms[row] = term
        stacked = jnp.stack([terms[row] for row in sorted(terms)]) * factor
        stacked = lax.psum(stacked, ("rows", "batch"))
        wide_r, wide_c = (3 - stacked.shape[0]) // 2, (3 - stacked.shape[1]) // 2
        kernel_grads[layer] = jnp.pad(
            stacked, ((wide_r, wide_r), (wide_c, wide_c), (0, 0), (0, 0))
        )
        dsignal = tap_backward(grad_flow, kernels[layer, 1], dilation)
        for row, band in fetch(grad_flow, spans[layer]):
            weights = (
                jnp.where(is_lower, kernels[layer, 2], kernels[layer, 0])
                if row is None
                else kernels[layer, 2 - row]
            )
            dsignal = dsignal + tap_backward(band, weights, dilation)
        _, back = jax.vjp(activate, layer_input.astype(jnp.float32))
        (dinput,) = back(dsignal)
        grad_flow = (grad_flow.astype(jnp.float32) + dinput).astype(jnp.bfloat16)
    return (current, grad_flow, jnp.stack(kernel_grads))


MESH = pl.DeviceIdType.MESH
CHUNKS = 4
FIRST_FLOWS, CORE_FLOWS, PLANE_FLOWS, LINE_FLOWS, LAST_FLOWS = ((0, 1), (2,), (), (), (3,))
FLAT = (((1,), (0,)), ((), ()))
TURNED = (((1,), (1,)), ((), ()))
SUMMED = (((0,), (0,)), ((), ()))


def normalise(values):
    scale = lax.rsqrt(jnp.mean(values * values, axis=-1, keepdims=True) + 1e-05)
    normed = values * scale
    gate = 1.0 / (1.0 + jnp.exp(-normed))
    return scale, normed, gate


def activate_back(values, dsignal):
    scale, normed, gate = normalise(values)
    dnormed = dsignal * (gate + normed * gate * (1.0 - gate))
    return scale * (dnormed - normed * jnp.mean(dnormed * normed, axis=-1, keepdims=True))


def moved(array, offset):
    if offset == 0:
        return array
    blank = jnp.zeros((array.shape[0], abs(offset), array.shape[2]), array.dtype)
    if offset > 0:
        return jnp.concatenate([array[:, offset:], blank], axis=1)
    return jnp.concatenate([blank, array[:, :offset]], axis=1)


def flat(array):
    return array.reshape(array.shape[0] * array.shape[1], array.shape[2])


def fused_kernel(
    dilations, features, kernels, cotangent, result, grad_features, gathered,
    weights, signal0, other0, signal1, signal2, flow2, flow1, other1, center, center1,
    parts, from_core, core_sum, from_plane, sum_common, sum_side, from_line, from_side,
    load_sem, swap_send, swap_recv, core_send, core_recv, plane_send, plane_recv,
    line_send, line_recv, side_send, side_recv, gline_send, gline_recv,
    gplane_send, gplane_recv, gcore_send, gcore_recv,
):
    band_rows, width, channels = features.shape
    step = band_rows // CHUNKS
    near, mid = dilations[0], dilations[1]
    row, batch = lax.axis_index("rows"), lax.axis_index("batch")
    line, across = lax.div(row, 2), lax.rem(row, 2)
    plane_y, core = lax.div(batch, 2), lax.rem(batch, 2)
    member = plane_y * 2 + across
    lower = lax.div(line, 2)
    side = lax.rem(line, 2)

    def toggled(value, bits):
        if bits == 1:
            return value + 1 - 2 * lax.rem(value, 2)
        if bits == 2:
            return lax.rem(value + 2, 4)
        return 3 - value

    def on_line(bits):
        return (toggled(line, bits) * 2 + across, batch)

    def on_plane(bits):
        other = toggled(member, bits)
        return (line * 2 + lax.rem(other, 2), lax.div(other, 2) * 2 + core)

    core_mate = (row, plane_y * 2 + 1 - core)
    swap_mate = on_line(2)

    loads = []
    first = 0
    for slot, (tap, taps) in enumerate(((0, 9), (12, 3), (22, 1))):
        copy = pltpu.make_async_copy(
            kernels.at[pl.ds(tap * channels, taps * channels)],
            weights.at[pl.ds(first * channels, taps * channels)],
            load_sem.at[slot],
        )
        copy.start()
        loads.append(copy)
        first += taps

    barrier = pltpu.get_barrier_semaphore()
    mates = [core_mate] + [on_line(k) for k in (1, 2, 3)] + [on_plane(k) for k in (1, 2, 3)]
    for mate in mates:
        pl.semaphore_signal(barrier, inc=1, device_id=mate, device_id_type=MESH)
    pl.semaphore_wait(barrier, len(mates))

    def remote(source, target, send, recv, mate):
        return pltpu.make_async_remote_copy(
            src_ref=source, dst_ref=target, send_sem=send, recv_sem=recv,
            device_id=mate, device_id_type=MESH,
        )

    def swap_signal(k):
        rows = pl.ds(k * step, step)
        return remote(
            signal0.at[rows], other0.at[rows], swap_send.at[k], swap_recv.at[k], swap_mate
        )

    def swap_flow(k):
        rows = pl.ds(k * step, step)
        return remote(
            flow1.at[rows], other1.at[rows],
            swap_send.at[CHUNKS + k], swap_recv.at[CHUNKS + k], swap_mate,
        )

    def dot(left, right, how):
        return lax.dot_general(left, right, how, preferred_element_type=jnp.float32)

    def wide(start):
        if isinstance(start, int):
            return weights[start * channels : (start + 3) * channels]
        return weights[pl.ds(pl.multiple_of(start * channels, channels), 3 * channels)]

    def forward(array, start, dilation):
        return dot(
            jnp.concatenate(
                [flat(moved(array, -dilation)), flat(array), flat(moved(array, dilation))], axis=1
            ),
            wide(start),
            FLAT,
        )

    def backward(array, start, dilation):
        taps = wide(start)
        total = dot(flat(array), taps[channels : 2 * channels], TURNED)
        total = total + dot(flat(moved(array, dilation)), taps[:channels], TURNED)
        return total + dot(flat(moved(array, -dilation)), taps[2 * channels :], TURNED)

    def each_chunk(body):
        def run(k, carry):
            body(k)
            return carry

        lax.fori_loop(0, CHUNKS, run, 0)

    def send_signal(k):
        rows = pl.ds(k * step, step)
        values = flat(features[rows].astype(jnp.float32))
        _, normed, gate = normalise(values)
        signal0[rows] = (normed * gate).astype(jnp.bfloat16).reshape(step, width, channels)
        swap_signal(k).start()

    each_chunk(send_signal)
    loads[0].wait()

    def own_forward(k):
        rows = pl.ds(k * step, step)
        total = forward(signal0[rows], 3, near)
        center[rows] = (flat(features[rows].astype(jnp.float32)) + total).reshape(
            step, width, channels
        )

    each_chunk(own_forward)
    loads[1].wait()
    loads[2].wait()

    def through(k, then=()):
        rows = pl.ds(k * step, step)
        shape = (step, width, channels)
        swap_signal(k).wait_recv()
        for sent_now in then:
            swap_flow(sent_now).start()
        upper = forward(other0[rows], (1 - lower) * 6, near)
        inner = (flat(center[rows]) + upper).astype(jnp.bfloat16).astype(jnp.float32)
        _, normed, gate = normalise(inner)
        signal = (normed * gate).astype(jnp.bfloat16).reshape(shape)
        signal1[rows] = signal
        deep = (inner + forward(signal, 9, mid)).astype(jnp.bfloat16).astype(jnp.float32)
        _, normed, gate = normalise(deep)
        signal = (normed * gate).astype(jnp.bfloat16)
        signal2[rows] = signal.reshape(shape)
        last = weights[12 * channels : 13 * channels]
        result[rows] = (deep + dot(signal, last, FLAT)).astype(jnp.bfloat16).reshape(shape)
        flow = cotangent[rows]
        dsignal = dot(flat(flow), last, TURNED)
        flow = (flat(flow.astype(jnp.float32)) + activate_back(deep, dsignal)).astype(jnp.bfloat16)
        flow = flow.reshape(shape)
        flow2[rows] = flow
        dsignal = backward(flow, 9, mid)
        flow = flat(flow.astype(jnp.float32)) + activate_back(inner, dsignal)
        flow1[rows] = flow.astype(jnp.bfloat16).reshape(shape)

    def run_through(k, carry):
        through(k)
        return carry

    lax.fori_loop(0, CHUNKS - 1, run_through, 0)
    through(CHUNKS - 1, FIRST_FLOWS)

    def keep(tap, terms):
        half, quarter = channels // 2, channels // 4
        terms = terms.astype(jnp.bfloat16)
        for h in range(2):
            for q in range(4):
                parts[h, q, tap] = terms[
                    q * quarter : (q + 1) * quarter, h * half : (h + 1) * half
                ]

    def gradient(source, flow, dilation, tap):
        if dilation is None:
            keep(tap, dot(flat(source), flat(flow), SUMMED))
            return
        for c in range(3):
            keep(tap + c, dot(flat(source), flat(moved(flow, (1 - c) * dilation)), SUMMED))

    gradient(signal2[...], cotangent[...], None, 6)
    gradient(signal1[...], flow2[...], mid, 3)
    gradient(signal0[...], flow1[...], near, 0)
    gradient(other0[...], flow1[...], near, 7)

    to_core = remote(parts.at[1 - core], from_core, core_send, core_recv, core_mate)
    to_core.start()
    for k in CORE_FLOWS:
        swap_flow(k).start()

    def own_backward(k):
        rows = pl.ds(k * step, step)
        center1[rows] = backward(flow1[rows], 3, near).reshape(step, width, channels)

    each_chunk(own_backward)

    def finish(k):
        rows = pl.ds(k * step, step)
        swap_flow(k).wait_recv()
        dsignal = flat(center1[rows]) + backward(other1[rows], lower * 6, near)
        flow = flat(flow1[rows].astype(jnp.float32))
        flow = flow + activate_back(flat(features[rows].astype(jnp.float32)), dsignal)
        grad_features[rows] = flow.astype(jnp.bfloat16).reshape(step, width, channels)

    to_core.wait_recv()
    core_sum[...] = (
        parts[core].astype(jnp.float32) + from_core[...].astype(jnp.float32)
    ).astype(jnp.bfloat16)
    to_plane = []
    for k in (1, 2, 3):
        copy = remote(
            core_sum.at[toggled(member, k)], from_plane.at[k - 1],
            plane_send.at[k - 1], plane_recv.at[k - 1], on_plane(k),
        )
        copy.start()
        to_plane.append(copy)
    for k in PLANE_FLOWS:
        swap_flow(k).start()

    finish(0)
    for copy in to_plane:
        copy.wait_recv()
    total = core_sum[member].astype(jnp.float32)
    for k in range(3):
        total = total + from_plane[k].astype(jnp.float32)
    total = total.astype(jnp.bfloat16)
    sum_common[...] = total[:7].reshape(sum_common.shape)
    sum_side[...] = total[7:].reshape(sum_side.shape)
    to_line = []
    for k in (1, 2, 3):
        copy = remote(
            sum_common.at[toggled(line, k)], from_line.at[k - 1],
            line_send.at[k - 1], line_recv.at[k - 1], on_line(k),
        )
        copy.start()
        to_line.append(copy)
    to_side = remote(sum_side.at[1 - side], from_side, side_send, side_recv, on_line(1))
    to_side.start()
    for k in LINE_FLOWS:
        swap_flow(k).start()

    finish(1)
    for copy in to_line:
        copy.wait_recv()
    to_side.wait_recv()
    common = sum_common.shape[1]
    total = sum_common[line].astype(jnp.float32)
    for k in range(3):
        total = total + from_line[k].astype(jnp.float32)
    mine = gathered.at[core, member, line]
    mine[:common] = total.astype(jnp.bfloat16)
    total = sum_side[side].astype(jnp.float32) + from_side[...].astype(jnp.float32)
    mine[common:] = total.astype(jnp.bfloat16)

    along_line = []
    for k in (1, 2, 3):
        copy = remote(mine, mine, gline_send.at[k - 1], gline_recv.at[k - 1], on_line(k))
        copy.start()
        along_line.append(copy)
    for k in LAST_FLOWS:
        swap_flow(k).start()
    finish(2)
    for copy in along_line:
        copy.wait_recv()
    quarter = gathered.at[core, member]
    across_core = []
    across_plane = []
    for k in (1, 2, 3):
        copy = remote(quarter, quarter, gplane_send.at[k - 1], gplane_recv.at[k - 1], on_plane(k))
        copy.start()
        across_plane.append(copy)
    copy = remote(quarter, quarter, gcore_send.at[0], gcore_recv.at[0], core_mate)
    copy.start()
    across_core.append(copy)
    finish(3)
    for k in (1, 2, 3):
        across_plane[k - 1].wait_recv()
        piece = gathered.at[core, toggled(member, k)]
        copy = remote(piece, piece, gcore_send.at[k], gcore_recv.at[k], core_mate)
        copy.start()
        across_core.append(copy)
    for copy in across_core:
        copy.wait_recv()
    for copy in [to_core, to_side] + to_plane + to_line + along_line + across_plane + across_core:
        copy.wait_send()

    def sent(k):
        swap_signal(k).wait_send()
        swap_flow(k).wait_send()

    each_chunk(sent)


def spread_kernel(
    factor, gathered, result, grad_features, out_result, out_features, out_kernels,
    pieces, sems,
):
    copies = [
        pltpu.make_async_copy(result, out_result, sems.at[0]),
        pltpu.make_async_copy(grad_features, out_features, sems.at[1]),
    ]
    for copy in copies:
        copy.start()
    quarter, half = gathered.shape[3] * 4 // 13, gathered.shape[4]
    common = 7 * quarter // 4
    sides = 3 * quarter // 2
    places = [None] * 13
    for tap in range(3):
        places[tap] = 3 + tap
        places[3 + tap] = 12 + tap
        places[7 + tap] = 6 + tap
        places[10 + tap] = tap
    places[6] = 22
    blank = pieces.at[13:16]
    blank[...] = jnp.zeros(blank.shape, jnp.float32)
    zeros = [(9, 3), (15, 3), (18, 3), (21, 1), (23, 1), (24, 3)]
    for slot, (tap, taps) in enumerate(zeros):
        copies.append(
            pltpu.make_async_copy(
                blank.at[:taps], out_kernels.at[pl.ds(tap, taps)], sems.at[2 + slot]
            )
        )
        copies[-1].start()
    for tap in range(13):
        for q in range(4):
            done = 0
            while done < quarter:
                if tap < 7:
                    spot, size = tap * quarter + done, common
                    line, start = spot // size, spot % size
                    offset = 0
                else:
                    upper, inner = (tap - 7) // 3, (tap - 7) % 3
                    spot, size = inner * quarter + done, sides
                    line, start = 2 * upper + spot // size, spot % size
                    offset = common
                rows = min(quarter - done, size - start)
                for h in range(2):
                    block = gathered[h, q, line, offset + start : offset + start + rows]
                    pieces[
                        tap,
                        q * quarter + done : q * quarter + done + rows,
                        h * half : (h + 1) * half,
                    ] = block.astype(jnp.float32) * factor
                done += rows
        copies.append(
            pltpu.make_async_copy(pieces.at[tap], out_kernels.at[places[tap]], sems.at[8 + tap])
        )
        copies[-1].start()
    for copy in copies:
        copy.wait()


def fused(features, kernels, cotangent):
    samples, band_rows, width, channels = features.shape
    dilations = [span * band_rows for span in SPANS]
    band = (band_rows, width, channels)
    low, full = jnp.bfloat16, jnp.float32
    half, quarter = channels // 2, channels // 4
    common, sides = 7 * quarter // 4, 3 * quarter // 2
    dma = pltpu.SemaphoreType.DMA
    vmem = pltpu.VMEM
    whole = pl.BlockSpec(memory_space=pltpu.VMEM)
    result, grad_features, gathered = pl.pallas_call(
        functools.partial(fused_kernel, dilations),
        out_shape=(
            jax.ShapeDtypeStruct(band, low),
            jax.ShapeDtypeStruct(band, low),
            jax.ShapeDtypeStruct((2, 4, 4, common + sides, half), low),
        ),
        in_specs=[whole, pl.BlockSpec(memory_space=pl.ANY), whole],
        out_specs=(whole, whole, whole),
        scratch_shapes=[
            vmem((13 * channels, channels), low),
            *[vmem(band, low) for _ in range(7)],
            vmem(band, full),
            vmem(band, full),
            vmem((2, 4, 10, quarter, half), low),
            vmem((4, 10, quarter, half), low),
            vmem((4, 10, quarter, half), low),
            vmem((3, 10, quarter, half), low),
            vmem((4, common, half), low),
            vmem((2, sides, half), low),
            vmem((3, common, half), low),
            vmem((sides, half), low),
            dma((3,)),
            dma((2 * CHUNKS,)),
            dma((2 * CHUNKS,)),
            dma, dma,
            dma((3,)), dma((3,)),
            dma((3,)), dma((3,)),
            dma, dma,
            dma((3,)), dma((3,)),
            dma((3,)), dma((3,)),
            dma((4,)), dma((4,)),
        ],
        compiler_params=pltpu.CompilerParams(
            collective_id=0, has_side_effects=True, vmem_limit_bytes=48 * 2**20
        ),
        cost_estimate=pl.CostEstimate(
            flops=48 * band_rows * width * channels * channels,
            bytes_accessed=10 * band_rows * width * channels,
            transcendentals=8 * band_rows * width * channels,
        ),
    )(
        features.reshape(band),
        kernels.reshape(27 * channels, channels),
        cotangent.reshape(band),
    )
    cells = samples * band_rows * width * lax.axis_size("rows") * lax.axis_size("batch")
    factor = 1.0 / math.sqrt(cells)
    anywhere = pl.BlockSpec(memory_space=pl.ANY)
    result, grad_features, terms = pl.pallas_call(
        functools.partial(spread_kernel, factor),
        out_shape=(
            jax.ShapeDtypeStruct(band, low),
            jax.ShapeDtypeStruct(band, low),
            jax.ShapeDtypeStruct((27, channels, channels), full),
        ),
        in_specs=[whole, anywhere, anywhere],
        out_specs=(anywhere, anywhere, anywhere),
        scratch_shapes=[vmem((16, channels, channels), full), dma((21,))],
        compiler_params=pltpu.CompilerParams(vmem_limit_bytes=16 * 2**20),
    )(gathered, result, grad_features)
    return (
        result.reshape(features.shape),
        grad_features.reshape(features.shape),
        terms.reshape(3, 3, 3, channels, channels),
    )


def one_swap(features):
    band_rows, width, channels = features.shape[1:]
    dilations = [span * band_rows for span in SPANS]
    return (
        features.shape[0] == 1
        and lax.axis_size("rows") == 2 * SPANS[0]
        and lax.axis_size("batch") == 4
        and SPANS[1] >= 2 * SPANS[0]
        and dilations[1] < width <= dilations[2]
        and band_rows % CHUNKS == 0
        and channels == 256
    )


def device_part(features, kernels, cotangent):
    if one_swap(features):
        return fused(features, kernels, cotangent)
    return local(features, kernels, cotangent)


def solution(mesh):
    placed = (P("batch", "rows", None, None), P(), P("batch", "rows", None, None))
    return jax.shard_map(
        device_part,
        mesh=mesh,
        in_specs=placed,
        out_specs=(P("batch", "rows", None, None), P("batch", "rows", None, None), P()),
        check_vma=False,
    )
```
